32 devices in a mesh: dp: 4 (over y, x), node: 4 (over z), dev: 2 (over core).
Axes of the slice: x: 2, y: 2, z: 4, core: 2. Of those that a mesh axis runs over, the one named last changes fastest.
Arguments:
- tokens: bfloat16 [4096, 3584], P(('dp', 'node', 'dev')), may hold values from -6 to 6
- cotangent: bfloat16 [4096, 3584], P(('dp', 'node', 'dev')), may hold values from -6 to 6
- routes: int32 [4096, 1], P(('dp', 'node', 'dev')), may hold values from 0 to 3; in each aligned block of 128 rows (0 to 127, 128 to 255, ...) at most 36 rows name the same one
- gates: float32 [4096, 1], P(('dp', 'node', 'dev')), may hold values from 0.05 to 1
- w_gate: bfloat16 [4, 3584, 1024], P('node', None, 'dev'), may hold values from -0.09375 to 0.09375
- w_up: bfloat16 [4, 3584, 1024], P('node', None, 'dev'), may hold values from -0.09375 to 0.09375
- w_down: bfloat16 [4, 1024, 3584], P('node', 'dev'), may hold values from -0.1875 to 0.1875
Outputs:
- mixed_out: bfloat16 [4096, 3584], P(('dp', 'node', 'dev'))
- grad_down: bfloat16 [4, 1024, 3584], P('node', 'dev')
The draws below stay inside these ranges and needn't reach their ends.
Inputs may be any that keep to these rules, and one draw needn't show every extreme that they name: `routes`: each token names 1 different experts; among the 128 tokens of one device at most 36 name any one expert, and in every draw some device has an expert named by exactly 36 of its tokens.
All inputs are finite; a program needn't handle non-finite values.
Results may differ from the reference program's by a relative error of at most 0.009.
Values may be sent and summed in bfloat16 or wider, within the bound.
No kernel may reach another device: no remote copies, remote signals or barrier semaphores. Data moves between devices by JAX's collectives and lax.ppermute only.
A program may use at most 64 MiB of HBM per device.

```python
import math
import jax
import jax.numpy as jnp
import numpy as np
from jax import lax

D = 3584
FH = 1024
TOP = 1
TOK = 128
EXPERTS = 4
FH_DEV = 512
CAP = 36
TOKENS = 4096
N_DP = 4
N_NODE = 4
N_DEV = 2


def steps_of(stream_key, shape, shards, smallest, high):
    loudness = 1.0
    for position, blocks in shards:
        draws = jax.random.uniform(jax.random.fold_in(jax.random.fold_in(stream_key, 6), position), (blocks,), jnp.float32, smallest / len(shards), high / len(shards))
        loudness = loudness * jnp.repeat(jnp.exp(draws), shape[position] // blocks).reshape((-1,) + (1,) * (len(shape) - 1 - position))
    return loudness


def assign_block(own_key, own, number, rows, amount, top, most, slope):
    sequence = jax.random.permutation(own_key, amount)
    packed, usual = shares(amount, rows * top, most, slope, True), shares(amount, rows * top, most, slope, False)
    places = jnp.arange(amount)

    def named(lengths, offset_by):
        used = int((lengths > 0).sum())
        fixed = max(1, used // 4)
        shifted = fixed + (places - fixed + offset_by * (used - fixed)) % max(1, amount - fixed)
        return jnp.zeros((amount,), jnp.int32).at[sequence[jnp.where(places < fixed, places, shifted)]].set(jnp.asarray(lengths, jnp.int32))

    lengths = jnp.where(number % 4 == 0, named(packed, number // 4), named(usual, number - number // 4 - 1))
    mixed = jax.random.permutation(jax.random.fold_in(own, 3), amount)
    giver, taker = mixed[0:amount // 2 * 2:2], mixed[1:amount // 2 * 2:2]
    margin = jnp.minimum(lengths[giver] - 1, most - lengths[taker]) // 2
    margin = jnp.where((giver == sequence[0]) | (taker == sequence[0]) | (lengths[taker] == 0), 0, jnp.maximum(margin, 0))
    shifted = jax.random.randint(jax.random.fold_in(own, 4), (amount // 2,), 0, 1 << 20) % (margin + 1)
    lengths = lengths.at[giver].add(-shifted).at[taker].add(shifted)
    members = jnp.searchsorted(jnp.cumsum(lengths), jnp.arange(rows * top), side="right").astype(jnp.int32)
    table = members.reshape(top, rows).T
    table = table[jax.random.permutation(jax.random.fold_in(own, 1), rows)]
    offset_by = jax.random.randint(jax.random.fold_in(own, 2), (rows, 1), 0, top)
    return jnp.take_along_axis(table, (jnp.arange(top)[None, :] + offset_by) % top, axis=1)


def shares(count, total, bound, lean, full):
    portions = [(1 << 20) // math.isqrt(grade ** lean) + 1 for grade in range(1, count + 1)]
    largest = bound if full else min(bound, max(-(-total // count), total * portions[0] // sum(portions)))
    least = 1 if total - largest >= count - 1 else 0
    given, surplus = [largest] + [least] * (count - 1), total - largest - least * (count - 1)
    while surplus > 0:
        candidates = [i for i in range(1, count) if given[i] < largest] or [i for i in range(1, count) if given[i] < bound]
        mass, remaining = sum([portions[i] for i in candidates]), surplus
        for i in candidates:
            addition = min(bound - given[i], max(1, remaining * portions[i] // mass), surplus)
            given[i] = given[i] + addition
            surplus = surplus - addition
    return np.array(given)


def scatter_about(rng, dims, width, limit, pieces=(), held_as=jnp.bfloat16):
    result = jax.random.normal(rng, dims, jnp.float32) * width
    if len(pieces) > 0:
        result = steps_of(rng, dims, pieces, -0.22, 0.18) * result
    return jnp.clip(result, min=-limit, max=limit).astype(held_as)


def setup_inputs(seed: int = 0) -> dict:
    keys = jax.random.split(jax.random.key(seed), 8)
    tokens = scatter_about(keys[0], (TOKENS, D), 1.0, 6.0, ((0, 32),))
    cotangent = scatter_about(keys[1], (TOKENS, D), 1.0, 6.0, ((0, 32),))
    routes_keys = jax.random.split(jax.random.fold_in(keys[2], 1), TOKENS // TOK)
    routes_turns = jax.random.permutation(jax.random.fold_in(keys[2], 3), TOKENS // TOK)
    routes = jax.vmap(lambda own, number: assign_block(jax.random.fold_in(keys[2], 2), own, number, TOK, EXPERTS, TOP, CAP, 2))(routes_keys, routes_turns).reshape((TOKENS, TOP))
    gates = jnp.clip(jnp.exp(math.log(1.0) - 2.9957323 * jax.random.uniform(keys[3], (TOKENS, TOP), jnp.float32) ** steps_of(keys[3], (TOKENS, TOP), ((0, 32),), -0.2, 0.2)), 0.05, 1.0)
    w_gate = scatter_about(keys[4], (EXPERTS, D, FH), D ** -0.5, 0.09375, ((0, 4), (2, 2)))
    w_up = scatter_about(keys[5], (EXPERTS, D, FH), D ** -0.5, 0.09375, ((0, 4), (2, 2)))
    w_down = scatter_about(keys[6], (EXPERTS, FH, D), FH ** -0.5, 0.1875, ((0, 4), (1, 2)))
    return {"tokens": tokens, "cotangent": cotangent, "routes": routes, "gates": gates, "w_gate": w_gate, "w_up": w_up, "w_down": w_down}


def reference(tokens, cotangent, routes, gates, w_gate, w_up, w_down):
    group_size = N_NODE * N_DEV
    replica_rows = group_size * TOK
    slot_count = group_size * CAP

    def replica_step(grad_total, replica):
        start = (replica * replica_rows).astype(jnp.int32)
        inputs = lax.dynamic_slice_in_dim(tokens, start, replica_rows, 0)
        grads = lax.dynamic_slice_in_dim(cotangent, start, replica_rows, 0)
        chosen = lax.dynamic_slice_in_dim(routes, start, replica_rows, 0).reshape(-1)
        weights = lax.dynamic_slice_in_dim(gates, start, replica_rows, 0).reshape(-1)
        mixed_acc = jnp.zeros((replica_rows, D), jnp.float32)
        for expert in range(EXPERTS):
            match = chosen == expert
            index = jnp.nonzero(match, size=slot_count, fill_value=0)[0].astype(jnp.int32)
            live = (jnp.arange(slot_count, dtype=jnp.int32) < jnp.sum(match.astype(jnp.int32))).astype(jnp.float32)
            token_index = index // TOP
            rows_in = inputs[token_index]
            scale = weights[index] * live
            weighted = (scale[:, None] * grads[token_index].astype(jnp.float32)).astype(jnp.bfloat16)
            gate_proj = jnp.dot(rows_in, w_gate[expert], preferred_element_type=jnp.float32)
            up_proj = jnp.dot(rows_in, w_up[expert], preferred_element_type=jnp.float32)
            hidden = (jax.nn.silu(gate_proj) * up_proj).astype(jnp.bfloat16)
            expert_out = jnp.zeros((slot_count, D), jnp.float32)
            for piece in range(N_DEV):
                lower = piece * FH_DEV
                partial_value = jnp.dot(hidden[:, lower:lower + FH_DEV], w_down[expert, lower:lower + FH_DEV], preferred_element_type=jnp.float32)
                expert_out = expert_out + lax.optimization_barrier(partial_value.astype(jnp.bfloat16)).astype(jnp.float32)
            expert_out = lax.optimization_barrier(expert_out.astype(jnp.bfloat16)).astype(jnp.float32)
            mixed_acc = mixed_acc.at[token_index].add(scale[:, None] * expert_out)
            grad_part = jnp.dot(hidden.T, weighted, preferred_element_type=jnp.float32)
            grad_part = lax.optimization_barrier(grad_part.astype(jnp.bfloat16)).astype(jnp.float32)
            grad_total = grad_total.at[expert].add(grad_part)
        return grad_total, mixed_acc.astype(jnp.bfloat16)

    grad_init = jnp.zeros((EXPERTS, FH, D), jnp.float32)
    grad_total, mixed_blocks = lax.scan(replica_step, grad_init, jnp.arange(N_DP, dtype=jnp.int32))
    return mixed_blocks.reshape(TOKENS, D), grad_total.astype(jnp.bfloat16)
```

```python
import functools

import jax
import jax.numpy as jnp
from jax import lax
from jax.experimental import pallas as pl
from jax.experimental.pallas import tpu as pltpu
from jax.sharding import PartitionSpec as P

BF = jnp.bfloat16
F32 = jnp.float32
QUARTERS = 4
NODES = 4
PARAMS = pltpu.CompilerParams(vmem_limit_bytes=40 * 1024 * 1024)


def sizes(capacity):
    main = capacity // 16 * 16
    return main, capacity - main


def dot(a, b):
    return jnp.dot(a, b, preferred_element_type=F32)


def iota(shape, dim):
    return lax.broadcasted_iota(jnp.int32, shape, dim)


def slots_of(routes, count):
    rel = routes ^ lax.axis_index("node")
    hits = jnp.where(iota((8, count), 0) == rel, 1.0, 0.0)
    earlier = jnp.where(iota((count, count), 0) < iota((count, count), 1), 1.0, 0.0)
    before = dot(hits.astype(BF), earlier.astype(BF))
    slot = jnp.sum(hits * before, axis=0, keepdims=True).astype(jnp.int32)
    return rel, slot


def codes_of(routes, count, main, rem):
    rel, slot = slots_of(routes, count)
    main_code = jnp.where(slot < main, rel * main + slot, -1)
    rem_code = jnp.where(slot >= main, rel * (QUARTERS * rem) + slot - main, -1000)
    return main_code, rem_code


def fold_kernel(main, rem, scaled, *refs):
    if scaled:
        routes_ref, gates_ref, rows_ref, *outs = refs
    else:
        routes_ref, rows_ref, *outs = refs
    count, width = rows_ref.shape
    piece = width // QUARTERS
    block = QUARTERS * rem
    main_code, rem_code = codes_of(routes_ref[...], count, main, rem)
    main_hot = iota((NODES * main, count), 0) == main_code
    main_mat = jnp.where(main_hot, 1.0, 0.0).astype(BF)
    if scaled:
        main_gate = jnp.sum(jnp.where(main_hot, gates_ref[...], 0.0), axis=1, keepdims=True)
    rest = jnp.zeros((NODES * block, piece), F32)
    for q in range(QUARTERS):
        columns = rows_ref[:, q * piece:(q + 1) * piece]
        value = dot(main_mat, columns)
        rem_hot = iota((NODES * block, count), 0) == rem_code + q * rem
        part = dot(jnp.where(rem_hot, 1.0, 0.0).astype(BF), columns)
        if scaled:
            value = value * main_gate
            part = part * jnp.sum(jnp.where(rem_hot, gates_ref[...], 0.0), axis=1, keepdims=True)
        rest = rest + part
        value = value.astype(BF)
        for p in range(NODES):
            outs[p][q * main:(q + 1) * main, :] = value[p * main:(p + 1) * main]
    rest = rest.astype(BF)
    for p in range(NODES):
        outs[p][QUARTERS * main:, :] = rest[p * block:(p + 1) * block]


def fold(routes_row, rows, gates_row, capacity):
    main, rem = sizes(capacity)
    count, width = rows.shape
    shape = (QUARTERS * capacity, width // QUARTERS)
    scaled = gates_row is not None
    args = (routes_row, gates_row, rows) if scaled else (routes_row, rows)
    return pl.pallas_call(
        functools.partial(fold_kernel, main, rem, scaled),
        out_shape=[jax.ShapeDtypeStruct(shape, BF)] * NODES,
        compiler_params=PARAMS,
        cost_estimate=pl.CostEstimate(flops=2 * count * count * width, bytes_accessed=4 * count * width, transcendentals=0),
    )(*args)


def unfold_matrix(rem, q, groups):
    block = QUARTERS * rem
    r, c = iota((groups * rem, groups * block), 0), iota((groups * rem, groups * block), 1)
    return jnp.where(c == (r // rem) * block + q * rem + r % rem, 1.0, 0.0).astype(BF)


def hidden_kernel(main, rem, *refs):
    folded, (gate_w, up_w, out_ref, gate_acc, up_acc) = refs[:2 * NODES], refs[2 * NODES:]
    q = pl.program_id(0)
    rows = pl.ds(pl.multiple_of(q * main, main), main)
    parts = []
    for h in range(2):
        half = folded[h * NODES:(h + 1) * NODES]
        parts += [ref[rows, :] for ref in half]
        rest = jnp.concatenate([ref[QUARTERS * main:, :] for ref in half], axis=0)
        parts.append(dot(unfold_matrix(rem, q, NODES), rest).astype(BF))
    x = jnp.concatenate(parts, axis=0)
    gate, up = dot(x, gate_w[0]), dot(x, up_w[0])

    @pl.when(q == 0)
    def _():
        gate_acc[...] = gate
        up_acc[...] = up

    @pl.when(q > 0)
    def _():
        gate_acc[...] += gate
        up_acc[...] += up

    @pl.when(q == QUARTERS - 1)
    def _():
        v = gate_acc[...]
        out_ref[...] = (v / (1.0 + jnp.exp(-v)) * up_acc[...]).astype(BF)


def hidden_of(folded, w_gate, w_up, capacity):
    main, rem = sizes(capacity)
    rows, piece = folded[0].shape
    fh = w_gate.shape[2]
    total = 2 * NODES * capacity
    whole = pl.BlockSpec((rows, piece), lambda q: (0, 0))
    weight = pl.BlockSpec((1, piece, fh), lambda q: (0, q, 0))
    return pl.pallas_call(
        functools.partial(hidden_kernel, main, rem),
        grid=(QUARTERS,),
        in_specs=[whole] * (2 * NODES) + [weight, weight],
        out_specs=pl.BlockSpec((total, fh), lambda q: (0, 0)),
        out_shape=jax.ShapeDtypeStruct((total, fh), BF),
        scratch_shapes=[pltpu.VMEM((total, fh), F32)] * 2,
        compiler_params=PARAMS,
        cost_estimate=pl.CostEstimate(flops=4 * total * fh * piece * QUARTERS, bytes_accessed=4 * fh * piece * QUARTERS, transcendentals=total * fh),
    )(*folded, w_gate, w_up)


def down_kernel(main, rem, capacity, hidden_ref, w_ref, own_ref, other_ref):
    q = pl.program_id(0)
    block = QUARTERS * rem
    r, c = iota((NODES * block, NODES * rem), 0), iota((NODES * block, NODES * rem), 1)
    spread = ((r // block) * rem + r % rem == c) & ((r % block) // rem == q)
    spread = jnp.where(spread, 1.0, 0.0).astype(BF)
    for h, out in enumerate((own_ref, other_ref)):
        base = h * NODES * capacity
        top = hidden_ref[base:base + NODES * main, :]
        low = hidden_ref[base + NODES * main:base + NODES * capacity, :]
        low = dot(spread, low).astype(BF)
        value = dot(jnp.concatenate([top, low], axis=0), w_ref[0]).astype(BF)
        for p in range(NODES):
            out[p, pl.ds(pl.multiple_of(q * main, main), main), :] = value[p * main:(p + 1) * main]
            rest = value[NODES * main + p * block:NODES * main + (p + 1) * block]

            @pl.when(q == 0)
            def _():
                out[p, QUARTERS * main:, :] = rest

            @pl.when(q > 0)
            def _():
                out[p, QUARTERS * main:, :] += rest


def down_of(hidden, w_down, capacity):
    main, rem = sizes(capacity)
    fh, width = w_down.shape[1:]
    piece = width // QUARTERS
    shape = (NODES, QUARTERS * capacity, piece)
    out = pl.BlockSpec(shape, lambda q: (0, 0, 0))
    return pl.pallas_call(
        functools.partial(down_kernel, main, rem, capacity),
        grid=(QUARTERS,),
        in_specs=[pl.BlockSpec(hidden.shape, lambda q: (0, 0)), pl.BlockSpec((1, fh, piece), lambda q: (0, 0, q))],
        out_specs=[out, out],
        out_shape=[jax.ShapeDtypeStruct(shape, BF)] * 2,
        compiler_params=PARAMS,
        cost_estimate=pl.CostEstimate(flops=2 * hidden.shape[0] * fh * width, bytes_accessed=2 * fh * width, transcendentals=0),
    )(hidden, w_down)


def add_kernel(a_ref, b_ref, *outs):
    for p, out in enumerate(outs):
        out[...] = (a_ref[p].astype(F32) + b_ref[p].astype(F32)).astype(BF)


def add_parts(a, b):
    return pl.pallas_call(
        add_kernel,
        out_shape=[jax.ShapeDtypeStruct(a.shape[1:], BF)] * a.shape[0],
        compiler_params=PARAMS,
        cost_estimate=pl.CostEstimate(flops=a.size, bytes_accessed=6 * a.size, transcendentals=0),
    )(a, b)


def combine_kernel(main, rem, routes_ref, gates_ref, *refs):
    parts, out_ref = refs[:NODES], refs[NODES]
    count, width = out_ref.shape
    piece = width // QUARTERS
    block = QUARTERS * rem
    main_code, rem_code = codes_of(routes_ref[...], count, main, rem)
    main_hot = jnp.where(iota((NODES * main, count), 0) == main_code, 1.0, 0.0)
    diagonal = iota((count, count), 0) == iota((count, count), 1)
    gate = jnp.sum(jnp.where(diagonal, gates_ref[...], 0.0), axis=1, keepdims=True)
    rest = jnp.concatenate([ref[QUARTERS * main:, :] for ref in parts], axis=0)
    for q in range(QUARTERS):
        rem_hot = jnp.where(iota((NODES * block, count), 0) == rem_code + q * rem, 1.0, 0.0)
        hot = jnp.concatenate([main_hot, rem_hot], axis=0)
        rows = jnp.concatenate([ref[q * main:(q + 1) * main, :] for ref in parts] + [rest], axis=0)
        value = dot(hot.T.astype(BF), rows)
        out_ref[:, q * piece:(q + 1) * piece] = (gate * value).astype(BF)


def combine(routes_row, gates_row, parts, count, width, capacity):
    main, rem = sizes(capacity)
    return pl.pallas_call(
        functools.partial(combine_kernel, main, rem),
        out_shape=jax.ShapeDtypeStruct((count, width), BF),
        compiler_params=PARAMS,
        cost_estimate=pl.CostEstimate(flops=2 * count * count * width, bytes_accessed=4 * count * width, transcendentals=0),
    )(routes_row, gates_row, *parts)


def grad_kernel(main, rem, capacity, groups, *refs):
    hidden = refs[:groups // 2]
    tops, lows = refs[groups // 2:groups // 2 + groups * NODES], refs[groups // 2 + groups * NODES:-1]
    out_ref = refs[-1]
    q = pl.program_id(0)
    half = NODES * capacity
    select = unfold_matrix(rem, q, NODES)
    left, right = [], []
    for g in range(groups):
        h = hidden[g // 2]
        base = g % 2 * half
        left.append(h[base:base + NODES * main, :])
        right += [ref[...] for ref in tops[g * NODES:(g + 1) * NODES]]
    for g in range(groups):
        h = hidden[g // 2]
        base = g % 2 * half
        left.append(h[base + NODES * main:base + half, :])
        rest = jnp.concatenate([ref[...] for ref in lows[g * NODES:(g + 1) * NODES]], axis=0)
        right.append(dot(select, rest).astype(BF))
    left, right = jnp.concatenate(left, axis=0), jnp.concatenate(right, axis=0)
    value = lax.dot_general(left, right, (((0,), (0,)), ((), ())), preferred_element_type=F32)
    out_ref[0] = value.astype(BF)


def gradient(hidden, folded, capacity):
    main, rem = sizes(capacity)
    groups = len(folded) // NODES
    fh = hidden[0].shape[1]
    piece = folded[0].shape[1]
    block = QUARTERS * rem
    low_at = QUARTERS * main // block
    whole = pl.BlockSpec(hidden[0].shape, lambda q: (0, 0))
    top = pl.BlockSpec((main, piece), lambda q: (q, 0))
    low = pl.BlockSpec((block, piece), lambda q: (low_at, 0))
    return pl.pallas_call(
        functools.partial(grad_kernel, main, rem, capacity, groups),
        grid=(QUARTERS,),
        in_specs=[whole] * len(hidden) + [top] * len(folded) + [low] * len(folded),
        out_specs=pl.BlockSpec((1, fh, piece), lambda q: (0, 0, q)),
        out_shape=jax.ShapeDtypeStruct((1, fh, QUARTERS * piece), BF),
        compiler_params=PARAMS,
        cost_estimate=pl.CostEstimate(
            flops=2 * groups * NODES * capacity * fh * piece * QUARTERS,
            bytes_accessed=2 * piece * QUARTERS * (fh + groups * NODES * capacity), transcendentals=0),
    )(*hidden, *folded, *folded)


def by_xor(x, axis, k):
    return lax.ppermute(x, axis, [(i, i ^ k) for i in range(lax.axis_size(axis))])


def per_device(capacity, tokens, cotangent, routes, gates, w_gate, w_up, w_down):
    count, width = tokens.shape
    routes_row, gates_row = routes.reshape(1, count), gates.reshape(1, count)
    t = fold(routes_row, tokens, None, capacity)
    t_in = [t[0]] + [None] * (NODES - 1)
    for p in (3, 2, 1):
        t_in[p] = by_xor(t[p], "node", p)
    w = fold(routes_row, cotangent, gates_row, capacity)
    w_in = [w[0]] + [None] * (NODES - 1)
    for p in (1, 3, 2):
        w_in[p] = by_xor(w[p], "node", p)
    t_other = [by_xor(v, "dev", 1) for v in t_in]
    hidden = hidden_of(t_in + t_other, w_gate, w_up, capacity)
    own, other = down_of(hidden, w_down, capacity)
    results = add_parts(own, by_xor(other, "dev", 1))
    back = [results[0]] + [by_xor(results[p], "node", p) for p in range(1, NODES)]
    mixed_out = combine(routes_row, gates_row, back, count, width, capacity)
    replicas = [w_in, [None] * NODES, [None] * NODES, [None] * NODES]
    for p in range(NODES):
        replicas[1][p], replicas[2][p] = by_xor(w_in[p], "dp", 1), by_xor(w_in[p], "dp", 2)
        replicas[3][p] = by_xor(replicas[1][p], "dp", 2) if p % 2 else by_xor(replicas[2][p], "dp", 1)
    folded = []
    for rows in replicas:
        folded += rows + [by_xor(v, "dev", 1) for v in rows]
    grad = gradient([hidden] + [by_xor(hidden, "dp", k) for k in (1, 2, 3)], folded, capacity)
    return mixed_out, grad


def plain_per_device(capacity, tokens, cotangent, routes, gates, w_gate, w_up, w_down):
    tok_count = tokens.shape[0]
    top_count = routes.shape[1]
    experts = w_gate.shape[0] * lax.axis_size("node")
    flat_routes = routes.reshape(-1)
    hits = (flat_routes[:, None] == jnp.arange(experts, dtype=jnp.int32)[None, :]).astype(jnp.int32)
    before = jnp.cumsum(hits, axis=0) - hits
    target = flat_routes * capacity + jnp.sum(before * hits, axis=1)
    placer = (target[:, None] == jnp.arange(experts * capacity, dtype=jnp.int32)[None, :]).astype(BF)
    token_rows = jnp.repeat(tokens, top_count, axis=0)
    weighted = (gates.reshape(-1)[:, None] * jnp.repeat(cotangent, top_count, axis=0).astype(F32)).astype(BF)
    swap = functools.partial(lax.all_to_all, axis_name="node", split_axis=0, concat_axis=0, tiled=True)
    gather = functools.partial(lax.all_gather, axis_name="dev", axis=0, tiled=True)

    def send(rows):
        placed = jnp.einsum("rs,rd->sd", placer, rows, preferred_element_type=F32).astype(BF)
        return gather(swap(placed.reshape(experts, capacity, -1)))

    all_inputs, all_grads = send(token_rows), send(weighted)
    gate_proj = jnp.einsum("scd,df->scf", all_inputs, w_gate[0], preferred_element_type=F32)
    up_proj = jnp.einsum("scd,df->scf", all_inputs, w_up[0], preferred_element_type=F32)
    hidden = (jax.nn.silu(gate_proj) * up_proj).astype(BF)
    partial_value = jnp.einsum("scf,fd->scd", hidden, w_down[0], preferred_element_type=F32)
    summed = lax.psum_scatter(partial_value.astype(BF), "dev", scatter_dimension=0, tiled=True)
    returned_rows = swap(summed)
    grad_part = jnp.einsum("scf,scd->fd", hidden, all_grads, preferred_element_type=F32)
    grad_total = lax.psum(grad_part.astype(BF), "dp")
    expert_out = jnp.dot(placer, returned_rows.reshape(experts * capacity, -1), preferred_element_type=F32)
    mixed_out = jnp.sum(gates[:, :, None] * expert_out.reshape(tok_count, top_count, -1), axis=1)
    return mixed_out.astype(BF), grad_total[None]


def solution(mesh):
    rows, columns = P(("dp", "node", "dev"), None), P("node", None, "dev")

    def program(tokens, cotangent, routes, gates, w_gate, w_up, w_down):
        nodes, cores, replicas = mesh.shape["node"], mesh.shape["dev"], mesh.shape["dp"]
        count, width = tokens.shape[0] // (nodes * cores * replicas), tokens.shape[1]
        experts = w_gate.shape[0]
        capacity = (count * routes.shape[1] * 9 + 8 * experts - 1) // (8 * experts)
        main, rem = sizes(capacity)
        small = nodes == NODES and replicas == 4 and cores == 2 and experts == nodes and routes.shape[1] == 1
        small = small and main > 0 and rem > 0 and (QUARTERS * rem) % 16 == 0 and main % (QUARTERS * rem) == 0
        small = small and width % (128 * QUARTERS) == 0 and count % 128 == 0
        return jax.shard_map(
            functools.partial(per_device if small else plain_per_device, capacity),
            mesh=mesh,
            in_specs=(rows, rows, rows, rows, columns, columns, P("node", "dev", None)),
            out_specs=(rows, P("node", "dev", None)),
            check_vma=False,
        )(tokens, cotangent, routes, gates, w_gate, w_up, w_down)

    return program
```

```python
import functools

import jax
import jax.numpy as jnp
from jax import lax
from jax.experimental import pallas as pl
from jax.experimental.pallas import tpu as pltpu
from jax.sharding import PartitionSpec as P

BF = jnp.bfloat16
F32 = jnp.float32
QUARTERS = 4
NODES = 4
PARAMS = pltpu.CompilerParams(vmem_limit_bytes=40 * 1024 * 1024)


def sizes(capacity):
    main = capacity // 16 * 16
    return main, capacity - main


def dot(a, b):
    return jnp.dot(a, b, preferred_element_type=F32)


def iota(shape, dim):
    return lax.broadcasted_iota(jnp.int32, shape, dim)


def slots_of(routes, count):
    rel = routes ^ lax.axis_index("node")
    hits = jnp.where(iota((8, count), 0) == rel, 1.0, 0.0)
    earlier = jnp.where(iota((count, count), 0) < iota((count, count), 1), 1.0, 0.0)
    before = dot(hits.astype(BF), earlier.astype(BF))
    slot = jnp.sum(hits * before, axis=0, keepdims=True).astype(jnp.int32)
    return rel, slot


def codes_of(routes, count, main, rem):
    rel, slot = slots_of(routes, count)
    main_code = jnp.where(slot < main, rel * main + slot, -1)
    rem_code = jnp.where(slot >= main, rel * (QUARTERS * rem) + slot - main, -1000)
    return main_code, rem_code


def fold_kernel(main, rem, scaled, *refs):
    if scaled:
        routes_ref, gates_ref, rows_ref, *outs = refs
    else:
        routes_ref, rows_ref, *outs = refs
    count, width = rows_ref.shape
    piece = width // QUARTERS
    block = QUARTERS * rem
    main_code, rem_code = codes_of(routes_ref[...], count, main, rem)
    main_hot = iota((NODES * main, count), 0) == main_code
    main_mat = jnp.where(main_hot, 1.0, 0.0).astype(BF)
    if scaled:
        main_gate = jnp.sum(jnp.where(main_hot, gates_ref[...], 0.0), axis=1, keepdims=True)
    rest = jnp.zeros((NODES * block, piece), F32)
    for q in range(QUARTERS):
        columns = rows_ref[:, q * piece:(q + 1) * piece]
        value = dot(main_mat, columns)
        rem_hot = iota((NODES * block, count), 0) == rem_code + q * rem
        part = dot(jnp.where(rem_hot, 1.0, 0.0).astype(BF), columns)
        if scaled:
            value = value * main_gate
            part = part * jnp.sum(jnp.where(rem_hot, gates_ref[...], 0.0), axis=1, keepdims=True)
        rest = rest + part
        value = value.astype(BF)
        for p in range(NODES):
            outs[p][q * main:(q + 1) * main, :] = value[p * main:(p + 1) * main]
    rest = rest.astype(BF)
    for p in range(NODES):
        outs[p][QUARTERS * main:, :] = rest[p * block:(p + 1) * block]


def fold(routes_row, rows, gates_row, capacity):
    main, rem = sizes(capacity)
    count, width = rows.shape
    shape = (QUARTERS * capacity, width // QUARTERS)
    scaled = gates_row is not None
    args = (routes_row, gates_row, rows) if scaled else (routes_row, rows)
    return pl.pallas_call(
        functools.partial(fold_kernel, main, rem, scaled),
        out_shape=[jax.ShapeDtypeStruct(shape, BF)] * NODES,
        compiler_params=PARAMS,
        cost_estimate=pl.CostEstimate(flops=2 * count * count * width, bytes_accessed=4 * count * width, transcendentals=0),
    )(*args)


def unfold_matrix(rem, q, groups):
    block = QUARTERS * rem
    r, c = iota((groups * rem, groups * block), 0), iota((groups * rem, groups * block), 1)
    return jnp.where(c == (r // rem) * block + q * rem + r % rem, 1.0, 0.0).astype(BF)


def hidden_kernel(main, rem, *refs):
    folded, (gate_w, up_w, out_ref, gate_acc, up_acc) = refs[:2 * NODES], refs[2 * NODES:]
    q = pl.program_id(0)
    rows = pl.ds(pl.multiple_of(q * main, main), main)
    parts = []
    for h in range(2):
        half = folded[h * NODES:(h + 1) * NODES]
        parts += [ref[rows, :] for ref in half]
        rest = jnp.concatenate([ref[QUARTERS * main:, :] for ref in half], axis=0)
        parts.append(dot(unfold_matrix(rem, q, NODES), rest).astype(BF))
    x = jnp.concatenate(parts, axis=0)
    gate, up = dot(x, gate_w[0]), dot(x, up_w[0])

    @pl.when(q == 0)
    def _():
        gate_acc[...] = gate
        up_acc[...] = up

    @pl.when(q > 0)
    def _():
        gate_acc[...] += gate
        up_acc[...] += up

    @pl.when(q == QUARTERS - 1)
    def _():
        v = gate_acc[...]
        out_ref[...] = (v / (1.0 + jnp.exp(-v)) * up_acc[...]).astype(BF)


def hidden_of(folded, w_gate, w_up, capacity):
    main, rem = sizes(capacity)
    rows, piece = folded[0].shape
    fh = w_gate.shape[2]
    total = 2 * NODES * capacity
    whole = pl.BlockSpec((rows, piece), lambda q: (0, 0))
    weight = pl.BlockSpec((1, piece, fh), lambda q: (0, q, 0))
    return pl.pallas_call(
        functools.partial(hidden_kernel, main, rem),
        grid=(QUARTERS,),
        in_specs=[whole] * (2 * NODES) + [weight, weight],
        out_specs=pl.BlockSpec((total, fh), lambda q: (0, 0)),
        out_shape=jax.ShapeDtypeStruct((total, fh), BF),
        scratch_shapes=[pltpu.VMEM((total, fh), F32)] * 2,
        compiler_params=PARAMS,
        cost_estimate=pl.CostEstimate(flops=4 * total * fh * piece * QUARTERS, bytes_accessed=4 * fh * piece * QUARTERS, transcendentals=total * fh),
    )(*folded, w_gate, w_up)


def down_kernel(main, rem, capacity, hidden_ref, w_ref, own_ref, other_ref):
    q = pl.program_id(0)
    block = QUARTERS * rem
    r, c = iota((NODES * block, NODES * rem), 0), iota((NODES * block, NODES * rem), 1)
    spread = ((r // block) * rem + r % rem == c) & ((r % block) // rem == q)
    spread = jnp.where(spread, 1.0, 0.0).astype(BF)
    for h, out in enumerate((own_ref, other_ref)):
        base = h * NODES * capacity
        top = hidden_ref[base:base + NODES * main, :]
        low = hidden_ref[base + NODES * main:base + NODES * capacity, :]
        low = dot(spread, low).astype(BF)
        value = dot(jnp.concatenate([top, low], axis=0), w_ref[0]).astype(BF)
        for p in range(NODES):
            out[p, pl.ds(pl.multiple_of(q * main, main), main), :] = value[p * main:(p + 1) * main]
            rest = value[NODES * main + p * block:NODES * main + (p + 1) * block]

            @pl.when(q == 0)
            def _():
                out[p, QUARTERS * main:, :] = rest

            @pl.when(q > 0)
            def _():
                out[p, QUARTERS * main:, :] += rest


def down_of(hidden, w_down, capacity):
    main, rem = sizes(capacity)
    fh, width = w_down.shape[1:]
    piece = width // QUARTERS
    shape = (NODES, QUARTERS * capacity, piece)
    out = pl.BlockSpec(shape, lambda q: (0, 0, 0))
    return pl.pallas_call(
        functools.partial(down_kernel, main, rem, capacity),
        grid=(QUARTERS,),
        in_specs=[pl.BlockSpec(hidden.shape, lambda q: (0, 0)), pl.BlockSpec((1, fh, piece), lambda q: (0, 0, q))],
        out_specs=[out, out],
        out_shape=[jax.ShapeDtypeStruct(shape, BF)] * 2,
        compiler_params=PARAMS,
        cost_estimate=pl.CostEstimate(flops=2 * hidden.shape[0] * fh * width, bytes_accessed=2 * fh * width, transcendentals=0),
    )(hidden, w_down)


def add_kernel(a_ref, b_ref, *outs):
    for p, out in enumerate(outs):
        out[...] = (a_ref[p].astype(F32) + b_ref[p].astype(F32)).astype(BF)


def add_parts(a, b):
    return pl.pallas_call(
        add_kernel,
        out_shape=[jax.ShapeDtypeStruct(a.shape[1:], BF)] * a.shape[0],
        compiler_params=PARAMS,
        cost_estimate=pl.CostEstimate(flops=a.size, bytes_accessed=6 * a.size, transcendentals=0),
    )(a, b)


def combine_kernel(main, rem, routes_ref, gates_ref, *refs):
    parts, out_ref = refs[:NODES], refs[NODES]
    count, width = out_ref.shape
    piece = width // QUARTERS
    block = QUARTERS * rem
    main_code, rem_code = codes_of(routes_ref[...], count, main, rem)
    main_hot = jnp.where(iota((NODES * main, count), 0) == main_code, 1.0, 0.0)
    diagonal = iota((count, count), 0) == iota((count, count), 1)
    gate = jnp.sum(jnp.where(diagonal, gates_ref[...], 0.0), axis=1, keepdims=True)
    rest = jnp.concatenate([ref[QUARTERS * main:, :] for ref in parts], axis=0)
    for q in range(QUARTERS):
        rem_hot = jnp.where(iota((NODES * block, count), 0) == rem_code + q * rem, 1.0, 0.0)
        hot = jnp.concatenate([main_hot, rem_hot], axis=0)
        rows = jnp.concatenate([ref[q * main:(q + 1) * main, :] for ref in parts] + [rest], axis=0)
        value = dot(hot.T.astype(BF), rows)
        out_ref[:, q * piece:(q + 1) * piece] = (gate * value).astype(BF)


def combine(routes_row, gates_row, parts, count, width, capacity):
    main, rem = sizes(capacity)
    return pl.pallas_call(
        functools.partial(combine_kernel, main, rem),
        out_shape=jax.ShapeDtypeStruct((count, width), BF),
        compiler_params=PARAMS,
        cost_estimate=pl.CostEstimate(flops=2 * count * count * width, bytes_accessed=4 * count * width, transcendentals=0),
    )(routes_row, gates_row, *parts)


def grad_kernel(main, rem, capacity, groups, *refs):
    hidden = refs[:groups // 2]
    tops, lows = refs[groups // 2:groups // 2 + groups * NODES], refs[groups // 2 + groups * NODES:-1]
    out_ref = refs[-1]
    q = pl.program_id(0)
    half = NODES * capacity
    select = unfold_matrix(rem, q, NODES)
    left, right = [], []
    for g in range(groups):
        h = hidden[g // 2]
        base = g % 2 * half
        left.append(h[base:base + NODES * main, :])
        right += [ref[...] for ref in tops[g * NODES:(g + 1) * NODES]]
    for g in range(groups):
        h = hidden[g // 2]
        base = g % 2 * half
        left.append(h[base + NODES * main:base + half, :])
        rest = jnp.concatenate([ref[...] for ref in lows[g * NODES:(g + 1) * NODES]], axis=0)
        right.append(dot(select, rest).astype(BF))
    left, right = jnp.concatenate(left, axis=0), jnp.concatenate(right, axis=0)
    value = lax.dot_general(left, right, (((0,), (0,)), ((), ())), preferred_element_type=F32)
    out_ref[0] = value.astype(BF)


def gradient(hidden, folded, capacity):
    main, rem = sizes(capacity)
    groups = len(folded) // NODES
    fh = hidden[0].shape[1]
    piece = folded[0].shape[1]
    block = QUARTERS * rem
    low_at = QUARTERS * main // block
    whole = pl.BlockSpec(hidden[0].shape, lambda q: (0, 0))
    top = pl.BlockSpec((main, piece), lambda q: (q, 0))
    low = pl.BlockSpec((block, piece), lambda q: (low_at, 0))
    return pl.pallas_call(
        functools.partial(grad_kernel, main, rem, capacity, groups),
        grid=(QUARTERS,),
        in_specs=[whole] * len(hidden) + [top] * len(folded) + [low] * len(folded),
        out_specs=pl.BlockSpec((1, fh, piece), lambda q: (0, 0, q)),
        out_shape=jax.ShapeDtypeStruct((1, fh, QUARTERS * piece), BF),
        compiler_params=PARAMS,
        cost_estimate=pl.CostEstimate(
            flops=2 * groups * NODES * capacity * fh * piece * QUARTERS,
            bytes_accessed=2 * piece * QUARTERS * (fh + groups * NODES * capacity), transcendentals=0),
    )(*hidden, *folded, *folded)


def by_xor(x, axis, k):
    return lax.ppermute(x, axis, [(i, i ^ k) for i in range(lax.axis_size(axis))])


def after(x, *earlier):
    return lax.optimization_barrier((x, *earlier))[0]


def per_device(capacity, tokens, cotangent, routes, gates, w_gate, w_up, w_down):
    count, width = tokens.shape
    routes_row, gates_row = routes.reshape(1, count), gates.reshape(1, count)
    t = fold(routes_row, tokens, None, capacity)
    t_in = [t[0]] + [None] * (NODES - 1)
    for p in (3, 2, 1):
        t_in[p] = by_xor(t[p], "node", p)
    w = fold(routes_row, cotangent, gates_row, capacity)
    w_in = [w[0], by_xor(w[1], "node", 1), None, None]
    w_in[3] = by_xor(after(w[3], t_in[3], t_in[2]), "node", 3)
    w_in[2] = by_xor(after(w[2], w_in[3]), "node", 2)
    t_other = [by_xor(v, "dev", 1) for v in t_in]
    hidden = hidden_of(t_in + t_other, w_gate, w_up, capacity)
    own, other = down_of(hidden, w_down, capacity)
    results = add_parts(own, by_xor(other, "dev", 1))
    back = [results[0], by_xor(results[1], "node", 1)]
    back += [by_xor(after(results[p], w_in[2]), "node", p) for p in (2, 3)]
    mixed_out = combine(routes_row, gates_row, back, count, width, capacity)
    replicas = [w_in, [None] * NODES, [None] * NODES, [None] * NODES]
    for p in range(NODES):
        replicas[1][p], replicas[2][p] = by_xor(w_in[p], "dp", 1), by_xor(w_in[p], "dp", 2)
        replicas[3][p] = by_xor(replicas[1][p], "dp", 2) if p % 2 else by_xor(replicas[2][p], "dp", 1)
    folded = []
    for rows in replicas:
        folded += rows + [by_xor(v, "dev", 1) for v in rows]
    grad = gradient([hidden] + [by_xor(hidden, "dp", k) for k in (1, 2, 3)], folded, capacity)
    return mixed_out, grad


def plain_per_device(capacity, tokens, cotangent, routes, gates, w_gate, w_up, w_down):
    tok_count = tokens.shape[0]
    top_count = routes.shape[1]
    experts = w_gate.shape[0] * lax.axis_size("node")
    flat_routes = routes.reshape(-1)
    hits = (flat_routes[:, None] == jnp.arange(experts, dtype=jnp.int32)[None, :]).astype(jnp.int32)
    before = jnp.cumsum(hits, axis=0) - hits
    target = flat_routes * capacity + jnp.sum(before * hits, axis=1)
    placer = (target[:, None] == jnp.arange(experts * capacity, dtype=jnp.int32)[None, :]).astype(BF)
    token_rows = jnp.repeat(tokens, top_count, axis=0)
    weighted = (gates.reshape(-1)[:, None] * jnp.repeat(cotangent, top_count, axis=0).astype(F32)).astype(BF)
    swap = functools.partial(lax.all_to_all, axis_name="node", split_axis=0, concat_axis=0, tiled=True)
    gather = functools.partial(lax.all_gather, axis_name="dev", axis=0, tiled=True)

    def send(rows):
        placed = jnp.einsum("rs,rd->sd", placer, rows, preferred_element_type=F32).astype(BF)
        return gather(swap(placed.reshape(experts, capacity, -1)))

    all_inputs, all_grads = send(token_rows), send(weighted)
    gate_proj = jnp.einsum("scd,df->scf", all_inputs, w_gate[0], preferred_element_type=F32)
    up_proj = jnp.einsum("scd,df->scf", all_inputs, w_up[0], preferred_element_type=F32)
    hidden = (jax.nn.silu(gate_proj) * up_proj).astype(BF)
    partial_value = jnp.einsum("scf,fd->scd", hidden, w_down[0], preferred_element_type=F32)
    summed = lax.psum_scatter(partial_value.astype(BF), "dev", scatter_dimension=0, tiled=True)
    returned_rows = swap(summed)
    grad_part = jnp.einsum("scf,scd->fd", hidden, all_grads, preferred_element_type=F32)
    grad_total = lax.psum(grad_part.astype(BF), "dp")
    expert_out = jnp.dot(placer, returned_rows.reshape(experts * capacity, -1), preferred_element_type=F32)
    mixed_out = jnp.sum(gates[:, :, None] * expert_out.reshape(tok_count, top_count, -1), axis=1)
    return mixed_out.astype(BF), grad_total[None]


def solution(mesh):
    rows, columns = P(("dp", "node", "dev"), None), P("node", None, "dev")

    def program(tokens, cotangent, routes, gates, w_gate, w_up, w_down):
        nodes, cores, replicas = mesh.shape["node"], mesh.shape["dev"], mesh.shape["dp"]
        count, width = tokens.shape[0] // (nodes * cores * replicas), tokens.shape[1]
        experts = w_gate.shape[0]
        capacity = (count * routes.shape[1] * 9 + 8 * experts - 1) // (8 * experts)
        main, rem = sizes(capacity)
        small = nodes == NODES and replicas == 4 and cores == 2 and experts == nodes and routes.shape[1] == 1
        small = small and main > 0 and rem > 0 and (QUARTERS * rem) % 16 == 0 and main % (QUARTERS * rem) == 0
        small = small and width % (128 * QUARTERS) == 0 and count % 128 == 0
        return jax.shard_map(
            functools.partial(per_device if small else plain_per_device, capacity),
            mesh=mesh,
            in_specs=(rows, rows, rows, rows, columns, columns, P("node", "dev", None)),
            out_specs=(rows, P("node", "dev", None)),
            check_vma=False,
        )(tokens, cotangent, routes, gates, w_gate, w_up, w_down)

    return program
```

```python
import functools

import jax
import jax.numpy as jnp
from jax import lax
from jax.experimental import pallas as pl
from jax.experimental.pallas import tpu as pltpu
from jax.sharding import PartitionSpec as P

BF = jnp.bfloat16
F32 = jnp.float32
QUARTERS = 4
NODES = 4
PARAMS = pltpu.CompilerParams(vmem_limit_bytes=40 * 1024 * 1024)


def sizes(capacity):
    main = capacity // 16 * 16
    return main, capacity - main


def dot(a, b):
    return jnp.dot(a, b, preferred_element_type=F32)


def iota(shape, dim):
    return lax.broadcasted_iota(jnp.int32, shape, dim)


def slots_of(routes, count):
    rel = routes ^ lax.axis_index("node")
    hits = jnp.where(iota((8, count), 0) == rel, 1.0, 0.0)
    earlier = jnp.where(iota((count, count), 0) < iota((count, count), 1), 1.0, 0.0)
    before = dot(hits.astype(BF), earlier.astype(BF))
    slot = jnp.sum(hits * before, axis=0, keepdims=True).astype(jnp.int32)
    return rel, slot


def codes_of(routes, count, main, rem):
    rel, slot = slots_of(routes, count)
    main_code = jnp.where(slot < main, rel * main + slot, -1)
    rem_code = jnp.where(slot >= main, rel * (QUARTERS * rem) + slot - main, -1000)
    return main_code, rem_code


def fold_kernel(main, rem, scaled, *refs):
    if scaled:
        routes_ref, gates_ref, rows_ref, *outs = refs
    else:
        routes_ref, rows_ref, *outs = refs
    count, width = rows_ref.shape
    piece = width // QUARTERS
    block = QUARTERS * rem
    main_code, rem_code = codes_of(routes_ref[...], count, main, rem)
    main_hot = iota((NODES * main, count), 0) == main_code
    main_mat = jnp.where(main_hot, 1.0, 0.0).astype(BF)
    if scaled:
        main_gate = jnp.sum(jnp.where(main_hot, gates_ref[...], 0.0), axis=1, keepdims=True)
    rest = jnp.zeros((NODES * block, piece), F32)
    for q in range(QUARTERS):
        columns = rows_ref[:, q * piece:(q + 1) * piece]
        value = dot(main_mat, columns)
        rem_hot = iota((NODES * block, count), 0) == rem_code + q * rem
        part = dot(jnp.where(rem_hot, 1.0, 0.0).astype(BF), columns)
        if scaled:
            value = value * main_gate
            part = part * jnp.sum(jnp.where(rem_hot, gates_ref[...], 0.0), axis=1, keepdims=True)
        rest = rest + part
        value = value.astype(BF)
        for p in range(NODES):
            outs[p][q * main:(q + 1) * main, :] = value[p * main:(p + 1) * main]
    rest = rest.astype(BF)
    for p in range(NODES):
        outs[p][QUARTERS * main:, :] = rest[p * block:(p + 1) * block]


def fold(routes_row, rows, gates_row, capacity):
    main, rem = sizes(capacity)
    count, width = rows.shape
    shape = (QUARTERS * capacity, width // QUARTERS)
    scaled = gates_row is not None
    args = (routes_row, gates_row, rows) if scaled else (routes_row, rows)
    return pl.pallas_call(
        functools.partial(fold_kernel, main, rem, scaled),
        out_shape=[jax.ShapeDtypeStruct(shape, BF)] * NODES,
        compiler_params=PARAMS,
        cost_estimate=pl.CostEstimate(flops=2 * count * count * width, bytes_accessed=4 * count * width, transcendentals=0),
    )(*args)


def unfold_matrix(rem, q, groups):
    block = QUARTERS * rem
    r, c = iota((groups * rem, groups * block), 0), iota((groups * rem, groups * block), 1)
    return jnp.where(c == (r // rem) * block + q * rem + r % rem, 1.0, 0.0).astype(BF)


def hidden_kernel(main, rem, *refs):
    folded, (gate_w, up_w, out_ref, gate_acc, up_acc) = refs[:2 * NODES], refs[2 * NODES:]
    q = pl.program_id(0)
    rows = pl.ds(pl.multiple_of(q * main, main), main)
    parts = []
    for h in range(2):
        half = folded[h * NODES:(h + 1) * NODES]
        parts += [ref[rows, :] for ref in half]
        rest = jnp.concatenate([ref[QUARTERS * main:, :] for ref in half], axis=0)
        parts.append(dot(unfold_matrix(rem, q, NODES), rest).astype(BF))
    x = jnp.concatenate(parts, axis=0)
    gate, up = dot(x, gate_w[0]), dot(x, up_w[0])

    @pl.when(q == 0)
    def _():
        gate_acc[...] = gate
        up_acc[...] = up

    @pl.when(q > 0)
    def _():
        gate_acc[...] += gate
        up_acc[...] += up

    @pl.when(q == QUARTERS - 1)
    def _():
        v = gate_acc[...]
        out_ref[...] = (v / (1.0 + jnp.exp(-v)) * up_acc[...]).astype(BF)


def hidden_of(folded, w_gate, w_up, capacity):
    main, rem = sizes(capacity)
    rows, piece = folded[0].shape
    fh = w_gate.shape[2]
    total = 2 * NODES * capacity
    whole = pl.BlockSpec((rows, piece), lambda q: (0, 0))
    weight = pl.BlockSpec((1, piece, fh), lambda q: (0, q, 0))
    return pl.pallas_call(
        functools.partial(hidden_kernel, main, rem),
        grid=(QUARTERS,),
        in_specs=[whole] * (2 * NODES) + [weight, weight],
        out_specs=pl.BlockSpec((total, fh), lambda q: (0, 0)),
        out_shape=jax.ShapeDtypeStruct((total, fh), BF),
        scratch_shapes=[pltpu.VMEM((total, fh), F32)] * 2,
        compiler_params=pltpu.CompilerParams(vmem_limit_bytes=50 * 1024 * 1024),
        cost_estimate=pl.CostEstimate(flops=4 * total * fh * piece * QUARTERS, bytes_accessed=4 * fh * piece * QUARTERS, transcendentals=total * fh),
    )(*folded, w_gate, w_up)


def down_kernel(main, rem, capacity, hidden_ref, w_ref, own_ref, other_ref):
    q = pl.program_id(0)
    block = QUARTERS * rem
    r, c = iota((NODES * block, NODES * rem), 0), iota((NODES * block, NODES * rem), 1)
    spread = ((r // block) * rem + r % rem == c) & ((r % block) // rem == q)
    spread = jnp.where(spread, 1.0, 0.0).astype(BF)
    for h, out in enumerate((own_ref, other_ref)):
        base = h * NODES * capacity
        top = hidden_ref[base:base + NODES * main, :]
        low = hidden_ref[base + NODES * main:base + NODES * capacity, :]
        low = dot(spread, low).astype(BF)
        value = dot(jnp.concatenate([top, low], axis=0), w_ref[0]).astype(BF)
        for p in range(NODES):
            out[p, pl.ds(pl.multiple_of(q * main, main), main), :] = value[p * main:(p + 1) * main]
            rest = value[NODES * main + p * block:NODES * main + (p + 1) * block]

            @pl.when(q == 0)
            def _():
                out[p, QUARTERS * main:, :] = rest

            @pl.when(q > 0)
            def _():
                out[p, QUARTERS * main:, :] += rest


def down_of(hidden, w_down, capacity):
    main, rem = sizes(capacity)
    fh, width = w_down.shape[1:]
    piece = width // QUARTERS
    shape = (NODES, QUARTERS * capacity, piece)
    out = pl.BlockSpec(shape, lambda q: (0, 0, 0))
    return pl.pallas_call(
        functools.partial(down_kernel, main, rem, capacity),
        grid=(QUARTERS,),
        in_specs=[pl.BlockSpec(hidden.shape, lambda q: (0, 0)), pl.BlockSpec((1, fh, piece), lambda q: (0, 0, q))],
        out_specs=[out, out],
        out_shape=[jax.ShapeDtypeStruct(shape, BF)] * 2,
        compiler_params=PARAMS,
        cost_estimate=pl.CostEstimate(flops=2 * hidden.shape[0] * fh * width, bytes_accessed=2 * fh * width, transcendentals=0),
    )(hidden, w_down)


def add_kernel(a_ref, b_ref, *outs):
    for p, out in enumerate(outs):
        out[...] = (a_ref[p].astype(F32) + b_ref[p].astype(F32)).astype(BF)


def add_parts(a, b):
    return pl.pallas_call(
        add_kernel,
        out_shape=[jax.ShapeDtypeStruct(a.shape[1:], BF)] * a.shape[0],
        compiler_params=PARAMS,
        cost_estimate=pl.CostEstimate(flops=a.size, bytes_accessed=6 * a.size, transcendentals=0),
    )(a, b)


def combine_kernel(main, rem, routes_ref, gates_ref, *refs):
    parts, out_ref = refs[:NODES], refs[NODES]
    count, width = out_ref.shape
    piece = width // QUARTERS
    block = QUARTERS * rem
    main_code, rem_code = codes_of(routes_ref[...], count, main, rem)
    main_hot = jnp.where(iota((NODES * main, count), 0) == main_code, 1.0, 0.0)
    diagonal = iota((count, count), 0) == iota((count, count), 1)
    gate = jnp.sum(jnp.where(diagonal, gates_ref[...], 0.0), axis=1, keepdims=True)
    rest = jnp.concatenate([ref[QUARTERS * main:, :] for ref in parts], axis=0)
    for q in range(QUARTERS):
        rem_hot = jnp.where(iota((NODES * block, count), 0) == rem_code + q * rem, 1.0, 0.0)
        hot = jnp.concatenate([main_hot, rem_hot], axis=0)
        rows = jnp.concatenate([ref[q * main:(q + 1) * main, :] for ref in parts] + [rest], axis=0)
        value = dot(hot.T.astype(BF), rows)
        out_ref[:, q * piece:(q + 1) * piece] = (gate * value).astype(BF)


def combine(routes_row, gates_row, parts, count, width, capacity):
    main, rem = sizes(capacity)
    return pl.pallas_call(
        functools.partial(combine_kernel, main, rem),
        out_shape=jax.ShapeDtypeStruct((count, width), BF),
        compiler_params=PARAMS,
        cost_estimate=pl.CostEstimate(flops=2 * count * count * width, bytes_accessed=4 * count * width, transcendentals=0),
    )(routes_row, gates_row, *parts)


def grad_kernel(main, rem, capacity, groups, *refs):
    hidden = refs[:groups // 2]
    tops, lows = refs[groups // 2:groups // 2 + groups * NODES], refs[groups // 2 + groups * NODES:-1]
    out_ref = refs[-1]
    q = pl.program_id(0)
    half = NODES * capacity
    select = unfold_matrix(rem, q, NODES)
    left, right = [], []
    for g in range(groups):
        h = hidden[g // 2]
        base = g % 2 * half
        left.append(h[base:base + NODES * main, :])
        right += [ref[...] for ref in tops[g * NODES:(g + 1) * NODES]]
    for g in range(groups):
        h = hidden[g // 2]
        base = g % 2 * half
        left.append(h[base + NODES * main:base + half, :])
        rest = jnp.concatenate([ref[...] for ref in lows[g * NODES:(g + 1) * NODES]], axis=0)
        right.append(dot(select, rest).astype(BF))
    left, right = jnp.concatenate(left, axis=0), jnp.concatenate(right, axis=0)
    value = lax.dot_general(left, right, (((0,), (0,)), ((), ())), preferred_element_type=F32)
    out_ref[0] = value.astype(BF)


def gradient(hidden, folded, capacity):
    main, rem = sizes(capacity)
    groups = len(folded) // NODES
    fh = hidden[0].shape[1]
    piece = folded[0].shape[1]
    block = QUARTERS * rem
    low_at = QUARTERS * main // block
    whole = pl.BlockSpec(hidden[0].shape, lambda q: (0, 0))
    top = pl.BlockSpec((main, piece), lambda q: (q, 0))
    low = pl.BlockSpec((block, piece), lambda q: (low_at, 0))
    return pl.pallas_call(
        functools.partial(grad_kernel, main, rem, capacity, groups),
        grid=(QUARTERS,),
        in_specs=[whole] * len(hidden) + [top] * len(folded) + [low] * len(folded),
        out_specs=pl.BlockSpec((1, fh, piece), lambda q: (0, 0, q)),
        out_shape=jax.ShapeDtypeStruct((1, fh, QUARTERS * piece), BF),
        compiler_params=PARAMS,
        cost_estimate=pl.CostEstimate(
            flops=2 * groups * NODES * capacity * fh * piece * QUARTERS,
            bytes_accessed=2 * piece * QUARTERS * (fh + groups * NODES * capacity), transcendentals=0),
    )(*hidden, *folded, *folded)


def by_xor(x, axis, k):
    return lax.ppermute(x, axis, [(i, i ^ k) for i in range(lax.axis_size(axis))])


def after(x, *earlier):
    return lax.optimization_barrier((x, *earlier))[0]


def per_device(capacity, tokens, cotangent, routes, gates, w_gate, w_up, w_down):
    count, width = tokens.shape
    routes_row, gates_row = routes.reshape(1, count), gates.reshape(1, count)
    t = fold(routes_row, tokens, None, capacity)
    t_in = [t[0]] + [None] * (NODES - 1)
    for p in (3, 2, 1):
        t_in[p] = by_xor(t[p], "node", p)
    w = fold(routes_row, cotangent, gates_row, capacity)
    w_in = [w[0], by_xor(w[1], "node", 1), None, None]
    w_in[3] = by_xor(after(w[3], t_in[3], t_in[2]), "node", 3)
    w_in[2] = by_xor(after(w[2], w_in[3]), "node", 2)
    t_other = [by_xor(v, "dev", 1) for v in t_in]
    hidden = hidden_of(t_in + t_other, w_gate, w_up, capacity)
    own, other = down_of(hidden, w_down, capacity)
    results = add_parts(own, by_xor(other, "dev", 1))
    back = [results[0], by_xor(results[1], "node", 1)]
    back += [by_xor(after(results[p], w_in[2]), "node", p) for p in (2, 3)]
    mixed_out = combine(routes_row, gates_row, back, count, width, capacity)
    replicas = [w_in, [None] * NODES, [None] * NODES, [None] * NODES]
    for p in range(NODES):
        replicas[1][p], replicas[2][p] = by_xor(w_in[p], "dp", 1), by_xor(w_in[p], "dp", 2)
        replicas[3][p] = by_xor(replicas[1][p], "dp", 2) if p % 2 else by_xor(replicas[2][p], "dp", 1)
    folded = []
    for rows in replicas:
        folded += rows + [by_xor(v, "dev", 1) for v in rows]
    grad = gradient([hidden] + [by_xor(hidden, "dp", k) for k in (1, 2, 3)], folded, capacity)
    return mixed_out, grad


def plain_per_device(capacity, tokens, cotangent, routes, gates, w_gate, w_up, w_down):
    tok_count = tokens.shape[0]
    top_count = routes.shape[1]
    experts = w_gate.shape[0] * lax.axis_size("node")
    flat_routes = routes.reshape(-1)
    hits = (flat_routes[:, None] == jnp.arange(experts, dtype=jnp.int32)[None, :]).astype(jnp.int32)
    before = jnp.cumsum(hits, axis=0) - hits
    target = flat_routes * capacity + jnp.sum(before * hits, axis=1)
    placer = (target[:, None] == jnp.arange(experts * capacity, dtype=jnp.int32)[None, :]).astype(BF)
    token_rows = jnp.repeat(tokens, top_count, axis=0)
    weighted = (gates.reshape(-1)[:, None] * jnp.repeat(cotangent, top_count, axis=0).astype(F32)).astype(BF)
    swap = functools.partial(lax.all_to_all, axis_name="node", split_axis=0, concat_axis=0, tiled=True)
    gather = functools.partial(lax.all_gather, axis_name="dev", axis=0, tiled=True)

    def send(rows):
        placed = jnp.einsum("rs,rd->sd", placer, rows, preferred_element_type=F32).astype(BF)
        return gather(swap(placed.reshape(experts, capacity, -1)))

    all_inputs, all_grads = send(token_rows), send(weighted)
    gate_proj = jnp.einsum("scd,df->scf", all_inputs, w_gate[0], preferred_element_type=F32)
    up_proj = jnp.einsum("scd,df->scf", all_inputs, w_up[0], preferred_element_type=F32)
    hidden = (jax.nn.silu(gate_proj) * up_proj).astype(BF)
    partial_value = jnp.einsum("scf,fd->scd", hidden, w_down[0], preferred_element_type=F32)
    summed = lax.psum_scatter(partial_value.astype(BF), "dev", scatter_dimension=0, tiled=True)
    returned_rows = swap(summed)
    grad_part = jnp.einsum("scf,scd->fd", hidden, all_grads, preferred_element_type=F32)
    grad_total = lax.psum(grad_part.astype(BF), "dp")
    expert_out = jnp.dot(placer, returned_rows.reshape(experts * capacity, -1), preferred_element_type=F32)
    mixed_out = jnp.sum(gates[:, :, None] * expert_out.reshape(tok_count, top_count, -1), axis=1)
    return mixed_out.astype(BF), grad_total[None]


def solution(mesh):
    rows, columns = P(("dp", "node", "dev"), None), P("node", None, "dev")

    def program(tokens, cotangent, routes, gates, w_gate, w_up, w_down):
        nodes, cores, replicas = mesh.shape["node"], mesh.shape["dev"], mesh.shape["dp"]
        count, width = tokens.shape[0] // (nodes * cores * replicas), tokens.shape[1]
        experts = w_gate.shape[0]
        capacity = (count * routes.shape[1] * 9 + 8 * experts - 1) // (8 * experts)
        main, rem = sizes(capacity)
        small = nodes == NODES and replicas == 4 and cores == 2 and experts == nodes and routes.shape[1] == 1
        small = small and main > 0 and rem > 0 and (QUARTERS * rem) % 16 == 0 and main % (QUARTERS * rem) == 0
        small = small and width % (128 * QUARTERS) == 0 and count % 128 == 0
        return jax.shard_map(
            functools.partial(per_device if small else plain_per_device, capacity),
            mesh=mesh,
            in_specs=(rows, rows, rows, rows, columns, columns, P("node", "dev", None)),
            out_specs=(rows, P("node", "dev", None)),
            check_vma=False,
        )(tokens, cotangent, routes, gates, w_gate, w_up, w_down)

    return program
```
